32 devices in a mesh: sub: 16 (over z, y, x), grp: 2 (over core).
Axes of the slice: x: 2, y: 2, z: 4, core: 2. Of those that a mesh axis runs over, the one named last changes fastest.
Arguments:
- rhs_jump: float32 [16, 2, 256, 256], P('sub', 'grp'), may hold values from -6 to 6
- incision: int32 [16, 2, 256], P('sub', 'grp'), may hold values 0 or 1
- precond: float32 [16, 2, 256], P('sub', 'grp'), may hold values from 0.5 to 2
- left_rows: int32 [16, 2, 256], P('sub', 'grp'), may hold values from 0 to 1151, as said below
- right_rows: int32 [16, 2, 256], P('sub', 'grp'), may hold values from 0 to 1151, as said below
- diag_inv: float32 [16, 2, 3, 384, 384], P('sub', 'grp'), as said below
- coupling: float32 [16, 2, 2, 384, 384], P('sub', 'grp'), may hold values from -0.09185587 to 0.09185587
- coarse_basis: float32 [16, 2, 3, 384, 128], P('sub', 'grp'), may hold values from -0.25 to 0.25
- coarse_inv: float32 [16, 128, 128], P('sub'), as said below
Outputs:
- multipliers: float32 [16, 2, 256, 256], P('sub', 'grp')
- residual: float32 [16, 2, 256, 256], P('sub', 'grp')
The draws below stay inside these ranges and needn't reach their ends.
Inputs may be any that keep to these rules, and one draw needn't show every extreme that they name: `left_rows`: for each subdomain, its 256 left rows and 256 right rows are 512 distinct interior rows. `right_rows`: see left_rows. `diag_inv`: every block is invertible. `coarse_inv`: every block is symmetric positive definite.
All inputs are finite; a program needn't handle non-finite values. No bound on the sum of `incision` on one device may be relied on, other than what follows from the above.
Results may differ from the reference program's by a relative error of at most 0.0003.
Values sent between devices are 32-bit elements; how exact they have to be, the bound alone decides.
A program may use at most 64 MiB of HBM per device.

```python
import math
import jax
import jax.numpy as jnp
from jax import lax

BLK = 384
NB = 3
IFACE = 256
PRIMAL = 128
RHS = 256
ITERS = 3
SUBS = 16
GROUPS = 2


def interface_rows(key):
    base = jax.random.fold_in(key, 7)
    subkeys = jax.random.split(base, SUBS * GROUPS)

    def pick_rows(subkey):
        return jax.random.permutation(subkey, NB * BLK)[:2 * IFACE]
    picks = jax.vmap(pick_rows)(subkeys)
    return picks.reshape(SUBS, GROUPS, 2 * IFACE).astype(jnp.int32)


def draw_left_rows(key, part):
    return interface_rows(key)[:, :, :IFACE]


def draw_right_rows(key, part):
    return interface_rows(key)[:, :, IFACE:]


def draw_diag_inv(key, part):
    first, second = jax.random.split(jax.random.fold_in(key, 11))
    scales = jnp.exp(jax.random.uniform(first, (SUBS, GROUPS, NB, BLK), jnp.float32, 0.0, 0.693))
    noise = 0.25 * jax.random.normal(second, (SUBS, GROUPS, NB, BLK, BLK), jnp.float32) / BLK ** 0.5
    ident = jnp.eye(BLK, dtype=jnp.float32)
    return noise + scales[..., None] * ident


def draw_coarse_inv(key, part):
    first, second = jax.random.split(jax.random.fold_in(key, 13))
    factor = jax.random.normal(first, (SUBS, PRIMAL, PRIMAL), jnp.float32)
    diagonal = jnp.exp(jax.random.uniform(second, (SUBS, PRIMAL), jnp.float32, -0.693, 0.693))
    gram = jnp.einsum('spk,sqk->spq', factor, factor) * (0.5 / PRIMAL)
    return gram + diagonal[..., None] * jnp.eye(PRIMAL, dtype=jnp.float32)


def with_ends(values, key, least, high):
    index_at = [jax.random.randint(jax.random.fold_in(key, axis), (), 0, length) for axis, length in enumerate(values.shape)]
    widest = values.shape.index(max(values.shape))
    next_to = index_at[:widest] + [(index_at[widest] + 1) % values.shape[widest]] + index_at[widest + 1:]
    return values.at[tuple(index_at)].set(least).at[tuple(next_to)].set(high)


def block_scale(key, dims, cuts, least, high):
    level = 1.0
    for axis_at, blocks in cuts:
        draws = jax.random.uniform(jax.random.fold_in(jax.random.fold_in(key, 6), axis_at), (blocks,), jnp.float32, least / len(cuts), high / len(cuts))
        level = level * jnp.repeat(jnp.exp(draws), dims[axis_at] // blocks).reshape((-1,) + (1,) * (len(dims) - 1 - axis_at))
    return level


def bell_draw(key, shape, deviation, limit, shards=(), held_as=jnp.bfloat16):
    loudness = block_scale(key, shape, shards, -0.22, 0.18) if shards else 1.0
    entries = jax.random.normal(key, shape, jnp.float32) * deviation * loudness
    return jnp.minimum(jnp.maximum(entries, -limit), limit).astype(held_as)


def setup_inputs(seed: int = 0) -> dict:
    key_list = jax.random.split(jax.random.key(seed), 10)
    rhs_jump = bell_draw(key_list[0], (SUBS, GROUPS, IFACE, RHS), 1.0, 6.0, ((0, 16), (1, 2)), jnp.float32)
    incision = with_ends((jax.random.randint(key_list[1], (SUBS, GROUPS, IFACE), 0, 8) < 7).astype(jnp.int32), jax.random.fold_in(key_list[1], 1), 0, 1)
    precond = jnp.clip(jnp.exp(math.log(2.0) - 1.3862944 * jax.random.uniform(key_list[2], (SUBS, GROUPS, IFACE), jnp.float32) ** block_scale(key_list[2], (SUBS, GROUPS, IFACE), ((0, 16), (1, 2)), -0.2, 0.2)), 0.5, 2.0)
    left_rows = draw_left_rows(jax.random.fold_in(key_list[9], 71), 0)
    right_rows = draw_right_rows(jax.random.fold_in(key_list[9], 71), 0)
    diag_inv = draw_diag_inv(jax.random.fold_in(key_list[9], 71), 0)
    coupling = bell_draw(key_list[6], (SUBS, GROUPS, NB - 1, BLK, BLK), (0.3 / BLK ** 0.5), 0.09185587, ((0, 16), (1, 2)), jnp.float32)
    coarse_basis = bell_draw(key_list[7], (SUBS, GROUPS, NB, BLK, PRIMAL), (2 * IFACE) ** -0.5, 0.25, ((0, 16), (1, 2)), jnp.float32)
    coarse_inv = draw_coarse_inv(jax.random.fold_in(key_list[9], 71), 0)
    return {"rhs_jump": rhs_jump, "incision": incision, "precond": precond, "left_rows": left_rows, "right_rows": right_rows, "diag_inv": diag_inv, "coupling": coupling, "coarse_basis": coarse_basis, "coarse_inv": coarse_inv}


HIGH = lax.Precision.HIGHEST


def banded(dinv, coup, load):
    forward = []
    for block in range(NB):
        rhs_now = load[:, block]
        if block > 0:
            rhs_now = rhs_now - jnp.einsum("qab,qbr->qar", coup[:, block - 1], forward[-1], precision=HIGH)
        forward.append(jnp.einsum("qab,qbr->qar", dinv[:, block], rhs_now, precision=HIGH))
    backward = [None] * NB
    for block in range(NB - 1, -1, -1):
        rhs_now = forward[block]
        if block < NB - 1:
            rhs_now = rhs_now - jnp.einsum("qba,qbr->qar", coup[:, block], backward[block + 1], precision=HIGH)
        backward[block] = jnp.einsum("qba,qbr->qar", dinv[:, block], rhs_now, precision=HIGH)
    return jnp.stack(backward, axis=1)


def build_load(rrow, lrow, own, left):
    order = NB * BLK
    zeros = jnp.zeros((order, own.shape[1]), jnp.float32)
    return zeros.at[rrow].add(own).at[lrow].add(-left)


def reference(rhs_jump, incision, precond, left_rows, right_rows, diag_inv, coupling, coarse_basis, coarse_inv):
    count = SUBS * GROUPS
    order = NB * BLK
    cut = incision.astype(jnp.float32)[..., None]
    scaling = precond[..., None]
    lflat = left_rows.reshape(count, IFACE)
    rflat = right_rows.reshape(count, IFACE)
    dinv = diag_inv.reshape(count, NB, BLK, BLK)
    coup = coupling.reshape(count, NB - 1, BLK, BLK)
    basis = coarse_basis.reshape(count, order, PRIMAL)

    def apply(direc):
        left = jnp.roll(direc, 1, axis=0)
        load = jax.vmap(build_load)(rflat, lflat, direc.reshape(count, IFACE, RHS), left.reshape(count, IFACE, RHS))
        interior = banded(dinv, coup, load.reshape(count, NB, BLK, RHS)).reshape(count, order, RHS)
        wsum = jnp.einsum("qnp,qnr->qpr", basis, load, precision=HIGH).reshape(SUBS, GROUPS, PRIMAL, RHS).sum(axis=1)
        coarse = jnp.einsum("spk,skr->spr", coarse_inv, wsum, precision=HIGH)
        coarse_all = jnp.broadcast_to(coarse[:, None], (SUBS, GROUPS, PRIMAL, RHS)).reshape(count, PRIMAL, RHS)
        disp = interior + jnp.einsum("qnp,qpr->qnr", basis, coarse_all, precision=HIGH)
        yright = jax.vmap(lambda v, i: v[i])(disp, rflat).reshape(SUBS, GROUPS, IFACE, RHS)
        yleft = jax.vmap(lambda v, i: v[i])(disp, lflat).reshape(SUBS, GROUPS, IFACE, RHS)
        return cut * (yright - jnp.roll(yleft, -1, axis=0))

    def total(a, b):
        return jnp.sum(a * b, axis=(0, 1, 2))

    multipliers = jnp.zeros_like(rhs_jump)
    residual = cut * rhs_jump
    zvec = scaling * residual
    direc = zvec
    rz_now = total(residual, zvec)
    for step in range(ITERS):
        image = apply(direc)
        alpha = rz_now / total(direc, image)
        multipliers = multipliers + alpha * direc
        residual = residual - alpha * image
        if step + 1 < ITERS:
            zvec = scaling * residual
            rz_new = total(residual, zvec)
            direc = zvec + (rz_new / rz_now) * direc
            rz_now = rz_new
    return multipliers, residual
```

```python
import functools

import jax
import jax.numpy as jnp
from jax import lax
from jax.experimental import pallas as pl
from jax.experimental.pallas import tpu as pltpu
from jax.sharding import PartitionSpec as P

ROUNDS = 3
MESH = pl.DeviceIdType.MESH
F32 = jnp.float32
BF16 = jnp.bfloat16


def split(x):
    high = x.astype(BF16)
    return high, (x - high.astype(F32)).astype(BF16)


def dot(a, b, ca=1, cb=0):
    return lax.dot_general(a, b, (((ca,), (cb,)), ((), ())), preferred_element_type=F32)


def dot3(a, b, ca=1, cb=0):
    (ah, al), (bh, bl) = a, b
    return dot(ah, bh, ca, cb) + (dot(ah, bl, ca, cb) + dot(al, bh, ca, cb))


def kernel(
    subs, grps, inner, chunks,
    rhs, cut_in, pre_in, lrow, rrow, dinv, coup, basis, cinv,
    mult, resid,
    v0, w0, v2, upper, cuts, pres, smat, bet, bc, gmat,
    ysend, yrecv, usend, urecv, dsend, drecv, red, reda, redb, redm,
    s_v0, r_v0, s_cm, r_cm, s_up, r_up, s_dn, r_dn, s_u, r_u, s_a, r_a, s_b, r_b,
):
    sub, grp = lax.axis_index("sub"), lax.axis_index("grp")
    width = rhs.shape[0]
    cols = rhs.shape[1] // chunks
    nblk, blk = dinv.shape[0], dinv.shape[1]
    after = (lax.rem(sub + 1, subs), grp)
    before = (lax.rem(sub + subs - 1, subs), grp)
    plane = inner * grps
    outer = subs // inner
    at_plane = lax.rem(sub, inner) * grps + grp
    base = lax.div(sub, inner) * inner

    def plane_peer(j):
        idx = lax.rem(at_plane + j, plane)
        return (base + lax.div(idx, grps), lax.rem(idx, grps))

    def outer_peer(j):
        return (lax.rem(base + j * inner, subs) + lax.rem(sub, inner), grp)

    def grp_peer(j):
        return (sub, lax.rem(grp + j, grps))

    peers = [after, before]
    peers += [plane_peer(j) for j in range(1, plane)]
    peers += [outer_peer(j) for j in range(1, outer)]
    barrier = pltpu.get_barrier_semaphore()
    for peer in peers:
        pl.semaphore_signal(barrier, inc=1, device_id=peer, device_id_type=MESH)

    def send(src, dst, ssem, rsem, peer):
        copy = pltpu.make_async_remote_copy(
            src_ref=src, dst_ref=dst, send_sem=ssem, recv_sem=rsem, device_id=peer, device_id_type=MESH
        )
        copy.start()
        return copy

    def col(c):
        return slice(c * cols, (c + 1) * cols)

    eye = lax.broadcasted_iota(jnp.int32, (width, width), 0) == lax.broadcasted_iota(
        jnp.int32, (width, width), 1
    )

    def column(row):
        return jnp.broadcast_to(
            jnp.sum(jnp.where(eye, row, 0.0), axis=1, keepdims=True), (width, cols)
        )

    cut_row = cut_in[...].astype(F32)
    dsend[0:1, :] = cut_row
    dsend[1:2, :] = pre_in[...]
    cuts[:width, :] = column(cut_row)
    pres[:width, :] = column(pre_in[...])
    for c in range(chunks):
        v0[c, :width, :] = pres[:width, :] * (cuts[:width, :] * rhs[:, col(c)])
    pl.semaphore_wait(barrier, len(peers))
    sent = []
    cm_copy = send(dsend, drecv, s_cm, r_cm, after)
    v0_copy = [
        send(v0.at[c, pl.ds(0, width)], v0.at[c, pl.ds(width, width)], s_v0.at[c], r_v0.at[c], after)
        for c in range(chunks)
    ]
    sent += [cm_copy] + v0_copy

    index = jnp.concatenate([rrow[...], lrow[...]], axis=1)
    sign = jnp.where(
        lax.broadcasted_iota(jnp.int32, (1, 2 * width), 1) < width, 1.0, -1.0
    ).astype(F32)

    def chosen(k):
        rows = lax.broadcasted_iota(jnp.int32, (blk, 2 * width), 0) + k * blk
        return jnp.where(rows == index, sign, 0.0)

    total = None
    for k in range(nblk):
        pick = chosen(k)
        pick16 = pick.astype(BF16)
        bh, bl = split(basis[k])
        part = (dot(bh, pick16, 0, 0), dot(bl, pick16, 0, 0))
        total = part if total is None else (total[0] + part[0], total[1] + part[1])
        dh, dl = split(dinv[k])
        if k == 0:
            now = dot(dh, pick16) + dot(dl, pick16)
        else:
            last = (gmat[0, (k - 1) * blk:k * blk, :], gmat[1, (k - 1) * blk:k * blk, :])
            now = dot3((dh, dl), split(pick - dot3(split(coup[k - 1]), last)))
        nh, nl = split(now)
        gmat[0, k * blk:(k + 1) * blk, :] = nh
        gmat[1, k * blk:(k + 1) * blk, :] = nl
    bet[0] = total[0].astype(BF16)
    bet[1] = total[1].astype(BF16)
    bet_now = (bet[0], bet[1])
    bch, bcl = split(dot3(bet_now, split(cinv[...]), 0, 0))
    bc[0] = bch
    bc[1] = bcl
    gnow = (gmat[0], gmat[1])
    sh, sl = split(dot3(gnow, gnow, 0, 0) + dot3((bch, bcl), bet_now))
    smat[0] = sh
    smat[1] = sl

    cm_copy.wait_recv()
    cuts[width:, :] = column(drecv[0:1, :])
    pres[width:, :] = column(drecv[1:2, :])

    exchanges = {}

    def apply(step, c, vec):
        parts = split(vec)
        usend[step, c] = dot3((bet[0], bet[1]), parts)
        ucopies = [
            send(
                usend.at[step, c], urecv.at[step, c, j - 1],
                s_u.at[step, c, j - 1], r_u.at[step, c, j - 1], grp_peer(j),
            )
            for j in range(1, grps)
        ]
        out = dot3((smat[0], smat[1]), parts)
        others = None
        for j, copy in enumerate(ucopies):
            copy.wait_recv()
            others = urecv[step, c, j] if others is None else others + urecv[step, c, j]
        if others is not None:
            out = out + dot3((bc[0], bc[1]), split(others))
        ysend[step, c] = out
        lower, top = pl.ds(width, width), pl.ds(0, width)
        moves = [
            send(
                ysend.at[step, c, lower], yrecv.at[step, c, top],
                s_dn.at[step, c], r_dn.at[step, c], before,
            )
        ]
        if step + 1 < ROUNDS:
            moves.append(
                send(
                    ysend.at[step, c, top], yrecv.at[step, c, lower],
                    s_up.at[step, c], r_up.at[step, c], after,
                )
            )
        exchanges[step, c] = moves
        sent.extend(ucopies + moves)

    def image(step, c):
        for copy in exchanges[step, c]:
            copy.wait_recv()
        if step + 1 < ROUNDS:
            return cuts[...] * (ysend[step, c] + yrecv[step, c])
        return cuts[:width, :] * (ysend[step, c, :width, :] + yrecv[step, c, :width, :])

    def reduce(which):
        copies = [
            send(red.at[which], reda.at[which, j - 1], s_a.at[which, j - 1], r_a.at[which, j - 1], plane_peer(j))
            for j in range(1, plane)
        ]
        total = red[which]
        for j, copy in enumerate(copies):
            copy.wait_recv()
            total = total + reda[which, j]
        sent.extend(copies)
        if outer > 1:
            redm[which] = total
            copies = [
                send(redm.at[which], redb.at[which, j - 1], s_b.at[which, j - 1], r_b.at[which, j - 1], outer_peer(j))
                for j in range(1, outer)
            ]
            for j, copy in enumerate(copies):
                copy.wait_recv()
                total = total + redb[which, j]
            sent.extend(copies)
        return total

    def summed(a, b):
        return jnp.sum(a * b, axis=0, keepdims=True)

    red[...] = jnp.zeros_like(red)
    for c in range(chunks):
        v0_copy[c].wait_recv()
        apply(0, c, v0[c])
    for c in range(chunks):
        w = image(0, c)
        w0[c] = w
        v1 = pres[...] * w
        apply(1, c, v1)
        top = w[:width, :]
        r0 = cuts[:width, :] * rhs[:, col(c)]
        red[0, 0:1, col(c)] = summed(r0, v0[c, :width, :])
        red[0, 1:2, col(c)] = summed(top, v0[c, :width, :])
        red[0, 2:3, col(c)] = summed(top, v1[:width, :])
    first = reduce(0)
    alphas, betas = [], []
    for c in range(chunks):
        m0, m1, m2 = (first[i:i + 1, col(c)] for i in range(3))
        alpha = m0 / m1
        beta = (m0 - 2.0 * alpha * m1 + alpha * alpha * m2) / m0
        alphas.append(alpha)
        betas.append(beta)
        w1 = image(1, c)
        t1 = w0[c] - alpha * w1
        s1 = t1 + beta * w0[c]
        vnext = pres[...] * s1
        apply(2, c, vnext)
        wt = w0[c, :width, :]
        vt = v0[c, :width, :]
        t1, s1, vn = t1[:width, :], s1[:width, :], vnext[:width, :]
        z1 = vt - alpha * (pres[:width, :] * wt)
        r1 = cuts[:width, :] * rhs[:, col(c)] - alpha * wt
        d1 = z1 + beta * vt
        v2[c] = vn
        for i, kept in enumerate((t1, s1, z1, r1, d1)):
            upper[c, i] = kept
        pairs = ((r1, z1), (d1, s1), (s1, z1), (s1, vn), (z1, t1), (vn, t1))
        for i, (a, b) in enumerate(pairs):
            red[1, i:i + 1, col(c)] = summed(a, b)
    for c in range(chunks):
        w2 = image(2, c)
        w0[c, :width, :] = w2
        red[1, 6:7, col(c)] = summed(upper[c, 2], w2)
        red[1, 7:8, col(c)] = summed(v2[c], w2)
    second = reduce(1)
    for c in range(chunks):
        rz1, pi1, sz, sv, zt, vt1, zw, vw = (second[i:i + 1, col(c)] for i in range(8))
        alpha0 = alphas[c]
        alpha1 = rz1 / pi1
        rz2 = rz1 - 2.0 * alpha1 * sz + alpha1 * alpha1 * sv
        beta1 = rz2 / rz1
        pi2 = zt - alpha1 * (zw + vt1) + alpha1 * alpha1 * vw
        pi2 = pi2 + 2.0 * beta1 * (sz - alpha1 * sv) + beta1 * beta1 * pi1
        alpha2 = rz2 / pi2
        t1, s1, z1, r1, d1 = (upper[c, i] for i in range(5))
        d2 = z1 - alpha1 * v2[c] + beta1 * d1
        f2 = t1 - alpha1 * w0[c, :width, :] + beta1 * s1
        mult[:, col(c)] = alpha0 * v0[c, :width, :] + alpha1 * d1 + alpha2 * d2
        resid[:, col(c)] = r1 - alpha1 * s1 - alpha2 * f2
    for copy in sent:
        copy.wait_send()


def local(
    subs, grps,
    rhs_jump, incision, precond, left_rows, right_rows, diag_inv, coupling, coarse_basis, coarse_inv,
):
    width, loads = rhs_jump.shape[2:]
    nblk, blk = diag_inv.shape[2:4]
    primal = coarse_basis.shape[-1]
    order = nblk * blk
    inner = next(n for n in (4, 2, 1) if subs % n == 0)
    outer = subs // inner
    plane = inner * grps
    chunks = 2 if loads % 256 == 0 else 1
    cols = loads // chunks
    others = max(grps - 1, 1)
    dma = pltpu.SemaphoreType.DMA
    vmem = pltpu.VMEM
    scratch = [
        vmem((chunks, 2 * width, cols), F32),
        vmem((chunks, 2 * width, cols), F32),
        vmem((chunks, width, cols), F32),
        vmem((chunks, 5, width, cols), F32),
        vmem((2 * width, cols), F32),
        vmem((2 * width, cols), F32),
        vmem((2, 2 * width, 2 * width), BF16),
        vmem((2, primal, 2 * width), BF16),
        vmem((2, 2 * width, primal), BF16),
        vmem((2, order, 2 * width), BF16),
        vmem((ROUNDS, chunks, 2 * width, cols), F32),
        vmem((ROUNDS, chunks, 2 * width, cols), F32),
        vmem((ROUNDS, chunks, primal, cols), F32),
        vmem((ROUNDS, chunks, others, primal, cols), F32),
        vmem((8, width), F32),
        vmem((8, width), F32),
        vmem((2, 8, loads), F32),
        vmem((2, max(plane - 1, 1), 8, loads), F32),
        vmem((2, max(outer - 1, 1), 8, loads), F32),
        vmem((2, 8, loads), F32),
        dma((chunks,)), dma((chunks,)),
        dma, dma,
        dma((ROUNDS, chunks)), dma((ROUNDS, chunks)),
        dma((ROUNDS, chunks)), dma((ROUNDS, chunks)),
        dma((ROUNDS, chunks, others)), dma((ROUNDS, chunks, others)),
        dma((2, max(plane - 1, 1))), dma((2, max(plane - 1, 1))),
        dma((2, max(outer - 1, 1))), dma((2, max(outer - 1, 1))),
    ]
    shape = jax.ShapeDtypeStruct((width, loads), F32)
    mult, resid = pl.pallas_call(
        functools.partial(kernel, subs, grps, inner, chunks),
        out_shape=(shape, shape),
        in_specs=[pl.BlockSpec(memory_space=pltpu.VMEM)] * 9,
        out_specs=(pl.BlockSpec(memory_space=pltpu.VMEM),) * 2,
        scratch_shapes=scratch,
        compiler_params=pltpu.CompilerParams(
            collective_id=0, has_side_effects=True, vmem_limit_bytes=48 * 1024 * 1024
        ),
    )(
        rhs_jump[0, 0], incision[0], precond[0], left_rows[0], right_rows[0],
        diag_inv[0, 0], coupling[0, 0], coarse_basis[0, 0], coarse_inv[0],
    )
    return mult[None, None], resid[None, None]


def solution(mesh):
    sizes = dict(mesh.shape)
    placed = (
        P("sub", "grp", None, None),
        P("sub", "grp", None),
        P("sub", "grp", None),
        P("sub", "grp", None),
        P("sub", "grp", None),
        P("sub", "grp", None, None, None),
        P("sub", "grp", None, None, None),
        P("sub", "grp", None, None, None),
        P("sub", None, None),
    )
    return jax.shard_map(
        functools.partial(local, sizes["sub"], sizes["grp"]),
        mesh=mesh,
        in_specs=placed,
        out_specs=(P("sub", "grp", None, None), P("sub", "grp", None, None)),
        check_vma=False,
    )
```

```python
import functools

import jax
import jax.numpy as jnp
from jax import lax
from jax.experimental import pallas as pl
from jax.experimental.pallas import tpu as pltpu
from jax.sharding import PartitionSpec as P

ROUNDS = 3
MESH = pl.DeviceIdType.MESH
F32 = jnp.float32
BF16 = jnp.bfloat16


def split(x):
    high = x.astype(BF16)
    return high, (x - high.astype(F32)).astype(BF16)


def dot(a, b, ca=1, cb=0):
    return lax.dot_general(a, b, (((ca,), (cb,)), ((), ())), preferred_element_type=F32)


def dot3(a, b, ca=1, cb=0):
    (ah, al), (bh, bl) = a, b
    return dot(ah, bh, ca, cb) + (dot(ah, bl, ca, cb) + dot(al, bh, ca, cb))


def kernel(
    subs, grps, inner, chunks,
    *refs,
):
    ins, (mult, resid), held = refs[:9], refs[9:11], refs[11:20]
    s_in = refs[20]
    (
        v0, w0, v2, upper, cuts, pres, smat, bet, bc, gmat,
        ysend, yrecv, usend, urecv, dsend, drecv, red, reda, redb, redm,
        s_v0, r_v0, s_cm, r_cm, s_up, r_up, s_dn, r_dn, s_u, r_u, s_a, r_a, s_b, r_b,
    ) = refs[21:]
    rhs, cut_in, pre_in, lrow, rrow, dinv, coup, basis, cinv = held
    loads_in = [
        pltpu.make_async_copy(src, dst, s_in.at[i]) for i, (src, dst) in enumerate(zip(ins, held))
    ]
    for copy in loads_in:
        copy.start()
    sub, grp = lax.axis_index("sub"), lax.axis_index("grp")
    width = rhs.shape[0]
    cols = rhs.shape[1] // chunks
    nblk, blk = dinv.shape[0], dinv.shape[1]
    after = (lax.rem(sub + 1, subs), grp)
    before = (lax.rem(sub + subs - 1, subs), grp)
    plane = inner * grps
    outer = subs // inner
    at_plane = lax.rem(sub, inner) * grps + grp
    base = lax.div(sub, inner) * inner

    def plane_peer(j):
        idx = lax.rem(at_plane + j, plane)
        return (base + lax.div(idx, grps), lax.rem(idx, grps))

    def outer_peer(j):
        return (lax.rem(base + j * inner, subs) + lax.rem(sub, inner), grp)

    def grp_peer(j):
        return (sub, lax.rem(grp + j, grps))

    peers = [after, before]
    peers += [plane_peer(j) for j in range(1, plane)]
    peers += [outer_peer(j) for j in range(1, outer)]
    barrier = pltpu.get_barrier_semaphore()
    for peer in peers:
        pl.semaphore_signal(barrier, inc=1, device_id=peer, device_id_type=MESH)

    def send(src, dst, ssem, rsem, peer):
        copy = pltpu.make_async_remote_copy(
            src_ref=src, dst_ref=dst, send_sem=ssem, recv_sem=rsem, device_id=peer, device_id_type=MESH
        )
        copy.start()
        return copy

    def col(c):
        return slice(c * cols, (c + 1) * cols)

    eye = lax.broadcasted_iota(jnp.int32, (width, width), 0) == lax.broadcasted_iota(
        jnp.int32, (width, width), 1
    )

    def column(row):
        return jnp.broadcast_to(
            jnp.sum(jnp.where(eye, row, 0.0), axis=1, keepdims=True), (width, cols)
        )

    for copy in loads_in[:3]:
        copy.wait()
    cut_row = cut_in[...].astype(F32)
    dsend[0:1, :] = cut_row
    dsend[1:2, :] = pre_in[...]
    cuts[:width, :] = column(cut_row)
    pres[:width, :] = column(pre_in[...])
    for c in range(chunks):
        v0[c, :width, :] = pres[:width, :] * (cuts[:width, :] * rhs[:, col(c)])
    pl.semaphore_wait(barrier, len(peers))
    sent = []
    cm_copy = send(dsend, drecv, s_cm, r_cm, after)
    v0_copy = [
        send(v0.at[c, pl.ds(0, width)], v0.at[c, pl.ds(width, width)], s_v0.at[c], r_v0.at[c], after)
        for c in range(chunks)
    ]
    sent += [cm_copy] + v0_copy

    for copy in loads_in[3:]:
        copy.wait()
    index = jnp.concatenate([rrow[...], lrow[...]], axis=1)
    sign = jnp.where(
        lax.broadcasted_iota(jnp.int32, (1, 2 * width), 1) < width, 1.0, -1.0
    ).astype(F32)

    def chosen(k):
        rows = lax.broadcasted_iota(jnp.int32, (blk, 2 * width), 0) + k * blk
        return jnp.where(rows == index, sign, 0.0)

    total = None
    for k in range(nblk):
        pick = chosen(k)
        pick16 = pick.astype(BF16)
        bh, bl = split(basis[k])
        part = (dot(bh, pick16, 0, 0), dot(bl, pick16, 0, 0))
        total = part if total is None else (total[0] + part[0], total[1] + part[1])
        dh, dl = split(dinv[k])
        if k == 0:
            now = dot(dh, pick16) + dot(dl, pick16)
        else:
            last = (gmat[0, (k - 1) * blk:k * blk, :], gmat[1, (k - 1) * blk:k * blk, :])
            now = dot3((dh, dl), split(pick - dot3(split(coup[k - 1]), last)))
        nh, nl = split(now)
        gmat[0, k * blk:(k + 1) * blk, :] = nh
        gmat[1, k * blk:(k + 1) * blk, :] = nl
    bet[0] = total[0].astype(BF16)
    bet[1] = total[1].astype(BF16)
    bet_now = (bet[0], bet[1])
    bch, bcl = split(dot3(bet_now, split(cinv[...]), 0, 0))
    bc[0] = bch
    bc[1] = bcl
    gnow = (gmat[0], gmat[1])
    sh, sl = split(dot3(gnow, gnow, 0, 0) + dot3((bch, bcl), bet_now))
    smat[0] = sh
    smat[1] = sl

    cm_copy.wait_recv()
    cuts[width:, :] = column(drecv[0:1, :])
    pres[width:, :] = column(drecv[1:2, :])

    exchanges = {}

    def apply(step, c, vec):
        parts = split(vec)
        usend[step, c] = dot3((bet[0], bet[1]), parts)
        ucopies = [
            send(
                usend.at[step, c], urecv.at[step, c, j - 1],
                s_u.at[step, c, j - 1], r_u.at[step, c, j - 1], grp_peer(j),
            )
            for j in range(1, grps)
        ]
        out = dot3((smat[0], smat[1]), parts)
        others = None
        for j, copy in enumerate(ucopies):
            copy.wait_recv()
            others = urecv[step, c, j] if others is None else others + urecv[step, c, j]
        if others is not None:
            out = out + dot3((bc[0], bc[1]), split(others))
        ysend[step, c] = out
        lower, top = pl.ds(width, width), pl.ds(0, width)
        moves = [
            send(
                ysend.at[step, c, lower], yrecv.at[step, c, top],
                s_dn.at[step, c], r_dn.at[step, c], before,
            )
        ]
        if step + 1 < ROUNDS:
            moves.append(
                send(
                    ysend.at[step, c, top], yrecv.at[step, c, lower],
                    s_up.at[step, c], r_up.at[step, c], after,
                )
            )
        exchanges[step, c] = moves
        sent.extend(ucopies + moves)

    def image(step, c):
        for copy in exchanges[step, c]:
            copy.wait_recv()
        if step + 1 < ROUNDS:
            return cuts[...] * (ysend[step, c] + yrecv[step, c])
        return cuts[:width, :] * (ysend[step, c, :width, :] + yrecv[step, c, :width, :])

    def reduce(which):
        copies = [
            send(red.at[which], reda.at[which, j - 1], s_a.at[which, j - 1], r_a.at[which, j - 1], plane_peer(j))
            for j in range(1, plane)
        ]
        total = red[which]
        for j, copy in enumerate(copies):
            copy.wait_recv()
            total = total + reda[which, j]
        sent.extend(copies)
        if outer > 1:
            redm[which] = total
            copies = [
                send(redm.at[which], redb.at[which, j - 1], s_b.at[which, j - 1], r_b.at[which, j - 1], outer_peer(j))
                for j in range(1, outer)
            ]
            for j, copy in enumerate(copies):
                copy.wait_recv()
                total = total + redb[which, j]
            sent.extend(copies)
        return total

    def summed(a, b):
        return jnp.sum(a * b, axis=0, keepdims=True)

    red[...] = jnp.zeros_like(red)
    for c in range(chunks):
        v0_copy[c].wait_recv()
        apply(0, c, v0[c])
    for c in range(chunks):
        w = image(0, c)
        w0[c] = w
        v1 = pres[...] * w
        apply(1, c, v1)
        top = w[:width, :]
        r0 = cuts[:width, :] * rhs[:, col(c)]
        red[0, 0:1, col(c)] = summed(r0, v0[c, :width, :])
        red[0, 1:2, col(c)] = summed(top, v0[c, :width, :])
        red[0, 2:3, col(c)] = summed(top, v1[:width, :])
    first = reduce(0)
    alphas, betas = [], []
    for c in range(chunks):
        m0, m1, m2 = (first[i:i + 1, col(c)] for i in range(3))
        alpha = m0 / m1
        beta = (m0 - 2.0 * alpha * m1 + alpha * alpha * m2) / m0
        alphas.append(alpha)
        betas.append(beta)
        w1 = image(1, c)
        t1 = w0[c] - alpha * w1
        s1 = t1 + beta * w0[c]
        vnext = pres[...] * s1
        apply(2, c, vnext)
        wt = w0[c, :width, :]
        vt = v0[c, :width, :]
        t1, s1, vn = t1[:width, :], s1[:width, :], vnext[:width, :]
        z1 = vt - alpha * (pres[:width, :] * wt)
        r1 = cuts[:width, :] * rhs[:, col(c)] - alpha * wt
        d1 = z1 + beta * vt
        v2[c] = vn
        for i, kept in enumerate((t1, s1, z1, r1, d1)):
            upper[c, i] = kept
        pairs = ((r1, z1), (d1, s1), (s1, z1), (s1, vn), (z1, t1), (vn, t1))
        for i, (a, b) in enumerate(pairs):
            red[1, i:i + 1, col(c)] = summed(a, b)
    for c in range(chunks):
        w2 = image(2, c)
        w0[c, :width, :] = w2
        red[1, 6:7, col(c)] = summed(upper[c, 2], w2)
        red[1, 7:8, col(c)] = summed(v2[c], w2)
    second = reduce(1)
    for c in range(chunks):
        rz1, pi1, sz, sv, zt, vt1, zw, vw = (second[i:i + 1, col(c)] for i in range(8))
        alpha0 = alphas[c]
        alpha1 = rz1 / pi1
        rz2 = rz1 - 2.0 * alpha1 * sz + alpha1 * alpha1 * sv
        beta1 = rz2 / rz1
        pi2 = zt - alpha1 * (zw + vt1) + alpha1 * alpha1 * vw
        pi2 = pi2 + 2.0 * beta1 * (sz - alpha1 * sv) + beta1 * beta1 * pi1
        alpha2 = rz2 / pi2
        t1, s1, z1, r1, d1 = (upper[c, i] for i in range(5))
        d2 = z1 - alpha1 * v2[c] + beta1 * d1
        f2 = t1 - alpha1 * w0[c, :width, :] + beta1 * s1
        mult[:, col(c)] = alpha0 * v0[c, :width, :] + alpha1 * d1 + alpha2 * d2
        resid[:, col(c)] = r1 - alpha1 * s1 - alpha2 * f2
    for copy in sent:
        copy.wait_send()


def local(
    subs, grps,
    rhs_jump, incision, precond, left_rows, right_rows, diag_inv, coupling, coarse_basis, coarse_inv,
):
    width, loads = rhs_jump.shape[2:]
    nblk, blk = diag_inv.shape[2:4]
    primal = coarse_basis.shape[-1]
    order = nblk * blk
    inner = next(n for n in (4, 2, 1) if subs % n == 0)
    outer = subs // inner
    plane = inner * grps
    chunks = 2 if loads % 256 == 0 else 1
    cols = loads // chunks
    others = max(grps - 1, 1)
    dma = pltpu.SemaphoreType.DMA
    vmem = pltpu.VMEM
    given = (
        rhs_jump[0, 0], incision[0], precond[0], left_rows[0], right_rows[0],
        diag_inv[0, 0], coupling[0, 0], coarse_basis[0, 0], coarse_inv[0],
    )
    scratch = [vmem(array.shape, array.dtype) for array in given] + [dma((len(given),))]
    scratch += [
        vmem((chunks, 2 * width, cols), F32),
        vmem((chunks, 2 * width, cols), F32),
        vmem((chunks, width, cols), F32),
        vmem((chunks, 5, width, cols), F32),
        vmem((2 * width, cols), F32),
        vmem((2 * width, cols), F32),
        vmem((2, 2 * width, 2 * width), BF16),
        vmem((2, primal, 2 * width), BF16),
        vmem((2, 2 * width, primal), BF16),
        vmem((2, order, 2 * width), BF16),
        vmem((ROUNDS, chunks, 2 * width, cols), F32),
        vmem((ROUNDS, chunks, 2 * width, cols), F32),
        vmem((ROUNDS, chunks, primal, cols), F32),
        vmem((ROUNDS, chunks, others, primal, cols), F32),
        vmem((8, width), F32),
        vmem((8, width), F32),
        vmem((2, 8, loads), F32),
        vmem((2, max(plane - 1, 1), 8, loads), F32),
        vmem((2, max(outer - 1, 1), 8, loads), F32),
        vmem((2, 8, loads), F32),
        dma((chunks,)), dma((chunks,)),
        dma, dma,
        dma((ROUNDS, chunks)), dma((ROUNDS, chunks)),
        dma((ROUNDS, chunks)), dma((ROUNDS, chunks)),
        dma((ROUNDS, chunks, others)), dma((ROUNDS, chunks, others)),
        dma((2, max(plane - 1, 1))), dma((2, max(plane - 1, 1))),
        dma((2, max(outer - 1, 1))), dma((2, max(outer - 1, 1))),
    ]
    shape = jax.ShapeDtypeStruct((width, loads), F32)
    mult, resid = pl.pallas_call(
        functools.partial(kernel, subs, grps, inner, chunks),
        out_shape=(shape, shape),
        in_specs=[pl.BlockSpec(memory_space=pl.ANY)] * 9,
        out_specs=(pl.BlockSpec(memory_space=pltpu.VMEM),) * 2,
        scratch_shapes=scratch,
        compiler_params=pltpu.CompilerParams(
            collective_id=0, has_side_effects=True, vmem_limit_bytes=60 * 1024 * 1024
        ),
    )(*given)
    return mult[None, None], resid[None, None]


def solution(mesh):
    sizes = dict(mesh.shape)
    placed = (
        P("sub", "grp", None, None),
        P("sub", "grp", None),
        P("sub", "grp", None),
        P("sub", "grp", None),
        P("sub", "grp", None),
        P("sub", "grp", None, None, None),
        P("sub", "grp", None, None, None),
        P("sub", "grp", None, None, None),
        P("sub", None, None),
    )
    return jax.shard_map(
        functools.partial(local, sizes["sub"], sizes["grp"]),
        mesh=mesh,
        in_specs=placed,
        out_specs=(P("sub", "grp", None, None), P("sub", "grp", None, None)),
        check_vma=False,
    )
```

```python
import functools

import jax
import jax.numpy as jnp
from jax import lax
from jax.experimental import pallas as pl
from jax.experimental.pallas import tpu as pltpu
from jax.sharding import PartitionSpec as P

ROUNDS = 3
MESH = pl.DeviceIdType.MESH
F32 = jnp.float32
BF16 = jnp.bfloat16


def split(x):
    high = x.astype(BF16)
    return high, (x - high.astype(F32)).astype(BF16)


def dot(a, b, ca=1, cb=0):
    return lax.dot_general(a, b, (((ca,), (cb,)), ((), ())), preferred_element_type=F32)


def dot3(a, b, ca=1, cb=0):
    (ah, al), (bh, bl) = a, b
    return dot(ah, bh, ca, cb) + (dot(ah, bl, ca, cb) + dot(al, bh, ca, cb))


def kernel(
    subs, grps, inner, chunks,
    *refs,
):
    ins, (mult, resid), held = refs[:9], refs[9:11], refs[11:20]
    s_in = refs[20]
    (
        v0, w0, v2, upper, cuts, pres, smat, bet, bc, gmat,
        ysend, yrecv, usend, urecv, dsend, drecv, red, reda, redb, redm,
        s_v0, r_v0, s_cm, r_cm, s_up, r_up, s_dn, r_dn, s_u, r_u, s_a, r_a, s_b, r_b,
    ) = refs[21:]
    rhs, cut_in, pre_in, lrow, rrow, dinv, coup, basis, cinv = held
    loads_in = [
        pltpu.make_async_copy(src, dst, s_in.at[i]) for i, (src, dst) in enumerate(zip(ins, held))
    ]
    for copy in loads_in:
        copy.start()
    sub, grp = lax.axis_index("sub"), lax.axis_index("grp")
    width = rhs.shape[0]
    cols = rhs.shape[1] // chunks
    nblk, blk = dinv.shape[0], dinv.shape[1]
    after = (lax.rem(sub + 1, subs), grp)
    before = (lax.rem(sub + subs - 1, subs), grp)
    plane = inner * grps
    outer = subs // inner
    at_plane = lax.rem(sub, inner) * grps + grp
    base = lax.div(sub, inner) * inner

    def plane_peer(j):
        idx = lax.rem(at_plane + j, plane)
        return (base + lax.div(idx, grps), lax.rem(idx, grps))

    def outer_peer(j):
        return (lax.rem(base + j * inner, subs) + lax.rem(sub, inner), grp)

    def grp_peer(j):
        return (sub, lax.rem(grp + j, grps))

    peers = [after, before]
    peers += [plane_peer(j) for j in range(1, plane)]
    peers += [outer_peer(j) for j in range(1, outer)]
    barrier = pltpu.get_barrier_semaphore()
    for peer in peers:
        pl.semaphore_signal(barrier, inc=1, device_id=peer, device_id_type=MESH)

    def send(src, dst, ssem, rsem, peer):
        copy = pltpu.make_async_remote_copy(
            src_ref=src, dst_ref=dst, send_sem=ssem, recv_sem=rsem, device_id=peer, device_id_type=MESH
        )
        copy.start()
        return copy

    def col(c):
        return slice(c * cols, (c + 1) * cols)

    eye = lax.broadcasted_iota(jnp.int32, (width, width), 0) == lax.broadcasted_iota(
        jnp.int32, (width, width), 1
    )

    def column(row):
        return jnp.broadcast_to(
            jnp.sum(jnp.where(eye, row, 0.0), axis=1, keepdims=True), (width, cols)
        )

    for copy in loads_in[:3]:
        copy.wait()
    cut_row = cut_in[...].astype(F32)
    dsend[0:1, :] = cut_row
    dsend[1:2, :] = pre_in[...]
    cuts[:width, :] = column(cut_row)
    pres[:width, :] = column(pre_in[...])
    for c in range(chunks):
        v0[c, :width, :] = pres[:width, :] * (cuts[:width, :] * rhs[:, col(c)])
    pl.semaphore_wait(barrier, len(peers))
    sent = []
    cm_copy = send(dsend, drecv, s_cm, r_cm, after)
    v0_copy = [
        send(v0.at[c, pl.ds(0, width)], v0.at[c, pl.ds(width, width)], s_v0.at[c], r_v0.at[c], after)
        for c in range(chunks)
    ]
    sent += [cm_copy] + v0_copy

    for copy in loads_in[3:]:
        copy.wait()
    index = jnp.concatenate([rrow[...], lrow[...]], axis=1)
    sign = jnp.where(
        lax.broadcasted_iota(jnp.int32, (1, 2 * width), 1) < width, 1.0, -1.0
    ).astype(F32)

    def chosen(k):
        rows = lax.broadcasted_iota(jnp.int32, (blk, 2 * width), 0) + k * blk
        return jnp.where(rows == index, sign, 0.0)

    total = None
    for k in range(nblk):
        pick = chosen(k)
        pick16 = pick.astype(BF16)
        bh, bl = split(basis[k])
        part = (dot(bh, pick16, 0, 0), dot(bl, pick16, 0, 0))
        total = part if total is None else (total[0] + part[0], total[1] + part[1])
        dh, dl = split(dinv[k])
        if k == 0:
            now = dot(dh, pick16) + dot(dl, pick16)
        else:
            last = (gmat[0, (k - 1) * blk:k * blk, :], gmat[1, (k - 1) * blk:k * blk, :])
            now = dot3((dh, dl), split(pick - dot3(split(coup[k - 1]), last)))
        nh, nl = split(now)
        gmat[0, k * blk:(k + 1) * blk, :] = nh
        gmat[1, k * blk:(k + 1) * blk, :] = nl
    bet[0] = total[0].astype(BF16)
    bet[1] = total[1].astype(BF16)
    bet_now = (bet[0], bet[1])
    bch, bcl = split(dot3(bet_now, split(cinv[...]), 0, 0))
    bc[0] = bch
    bc[1] = bcl
    gnow = (gmat[0], gmat[1])
    sh, sl = split(dot3(gnow, gnow, 0, 0) + dot3((bch, bcl), bet_now))
    smat[0] = sh
    smat[1] = sl

    cm_copy.wait_recv()
    cuts[width:, :] = column(drecv[0:1, :])
    pres[width:, :] = column(drecv[1:2, :])

    exchanges = {}

    def apply(step, c, vec):
        parts = split(vec)
        usend[step, c] = dot3((bet[0], bet[1]), parts)
        ucopies = [
            send(
                usend.at[step, c], urecv.at[step, c, j - 1],
                s_u.at[step, c, j - 1], r_u.at[step, c, j - 1], grp_peer(j),
            )
            for j in range(1, grps)
        ]
        out = dot3((smat[0], smat[1]), parts)
        others = None
        for j, copy in enumerate(ucopies):
            copy.wait_recv()
            others = urecv[step, c, j] if others is None else others + urecv[step, c, j]
        if others is not None:
            out = out + dot3((bc[0], bc[1]), split(others))
        ysend[step, c] = out
        lower, top = pl.ds(width, width), pl.ds(0, width)
        moves = [
            send(
                ysend.at[step, c, lower], yrecv.at[step, c, top],
                s_dn.at[step, c], r_dn.at[step, c], before,
            )
        ]
        if step + 1 < ROUNDS:
            moves.append(
                send(
                    ysend.at[step, c, top], yrecv.at[step, c, lower],
                    s_up.at[step, c], r_up.at[step, c], after,
                )
            )
        exchanges[step, c] = moves
        sent.extend(ucopies + moves)

    def image(step, c):
        for copy in exchanges[step, c]:
            copy.wait_recv()
        if step + 1 < ROUNDS:
            return cuts[...] * (ysend[step, c] + yrecv[step, c])
        return cuts[:width, :] * (ysend[step, c, :width, :] + yrecv[step, c, :width, :])

    begun = {}

    def begin(which, c):
        here = pl.ds(c * cols, cols)
        begun[which, c] = [
            send(
                red.at[which, :, here], reda.at[which, j - 1, :, here],
                s_a.at[which, c, j - 1], r_a.at[which, c, j - 1], plane_peer(j),
            )
            for j in range(1, plane)
        ]
        sent.extend(begun[which, c])

    def finish(which):
        for c in range(chunks):
            for copy in begun[which, c]:
                copy.wait_recv()
        total = red[which]
        for j in range(plane - 1):
            total = total + reda[which, j]
        if outer > 1:
            redm[which] = total
            copies = [
                send(redm.at[which], redb.at[which, j - 1], s_b.at[which, j - 1], r_b.at[which, j - 1], outer_peer(j))
                for j in range(1, outer)
            ]
            for j, copy in enumerate(copies):
                copy.wait_recv()
                total = total + redb[which, j]
            sent.extend(copies)
        return total

    def summed(a, b):
        return jnp.sum(a * b, axis=0, keepdims=True)

    red[...] = jnp.zeros_like(red)
    for c in range(chunks):
        v0_copy[c].wait_recv()
        apply(0, c, v0[c])
    for c in range(chunks):
        w = image(0, c)
        w0[c] = w
        v1 = pres[...] * w
        top = w[:width, :]
        r0 = cuts[:width, :] * rhs[:, col(c)]
        red[0, 0:1, col(c)] = summed(r0, v0[c, :width, :])
        red[0, 1:2, col(c)] = summed(top, v0[c, :width, :])
        red[0, 2:3, col(c)] = summed(top, v1[:width, :])
        begin(0, c)
        apply(1, c, v1)
    first = finish(0)
    alphas, betas = [], []
    for c in range(chunks):
        m0, m1, m2 = (first[i:i + 1, col(c)] for i in range(3))
        alpha = m0 / m1
        beta = (m0 - 2.0 * alpha * m1 + alpha * alpha * m2) / m0
        alphas.append(alpha)
        betas.append(beta)
        w1 = image(1, c)
        t1 = w0[c] - alpha * w1
        s1 = t1 + beta * w0[c]
        vnext = pres[...] * s1
        apply(2, c, vnext)
        wt = w0[c, :width, :]
        vt = v0[c, :width, :]
        t1, s1, vn = t1[:width, :], s1[:width, :], vnext[:width, :]
        z1 = vt - alpha * (pres[:width, :] * wt)
        r1 = cuts[:width, :] * rhs[:, col(c)] - alpha * wt
        d1 = z1 + beta * vt
        v2[c] = vn
        for i, kept in enumerate((t1, s1, z1, r1, d1)):
            upper[c, i] = kept
        pairs = ((r1, z1), (d1, s1), (s1, z1), (s1, vn), (z1, t1), (vn, t1))
        for i, (a, b) in enumerate(pairs):
            red[1, i:i + 1, col(c)] = summed(a, b)
    for c in range(chunks):
        w2 = image(2, c)
        w0[c, :width, :] = w2
        red[1, 6:7, col(c)] = summed(upper[c, 2], w2)
        red[1, 7:8, col(c)] = summed(v2[c], w2)
        begin(1, c)
    second = finish(1)
    for c in range(chunks):
        rz1, pi1, sz, sv, zt, vt1, zw, vw = (second[i:i + 1, col(c)] for i in range(8))
        alpha0 = alphas[c]
        alpha1 = rz1 / pi1
        rz2 = rz1 - 2.0 * alpha1 * sz + alpha1 * alpha1 * sv
        beta1 = rz2 / rz1
        pi2 = zt - alpha1 * (zw + vt1) + alpha1 * alpha1 * vw
        pi2 = pi2 + 2.0 * beta1 * (sz - alpha1 * sv) + beta1 * beta1 * pi1
        alpha2 = rz2 / pi2
        t1, s1, z1, r1, d1 = (upper[c, i] for i in range(5))
        d2 = z1 - alpha1 * v2[c] + beta1 * d1
        f2 = t1 - alpha1 * w0[c, :width, :] + beta1 * s1
        mult[:, col(c)] = alpha0 * v0[c, :width, :] + alpha1 * d1 + alpha2 * d2
        resid[:, col(c)] = r1 - alpha1 * s1 - alpha2 * f2
    for copy in sent:
        copy.wait_send()


def local(
    subs, grps,
    rhs_jump, incision, precond, left_rows, right_rows, diag_inv, coupling, coarse_basis, coarse_inv,
):
    width, loads = rhs_jump.shape[2:]
    nblk, blk = diag_inv.shape[2:4]
    primal = coarse_basis.shape[-1]
    order = nblk * blk
    inner = next(n for n in (4, 2, 1) if subs % n == 0)
    outer = subs // inner
    plane = inner * grps
    chunks = 2 if loads % 256 == 0 else 1
    cols = loads // chunks
    others = max(grps - 1, 1)
    dma = pltpu.SemaphoreType.DMA
    vmem = pltpu.VMEM
    given = (
        rhs_jump[0, 0], incision[0], precond[0], left_rows[0], right_rows[0],
        diag_inv[0, 0], coupling[0, 0], coarse_basis[0, 0], coarse_inv[0],
    )
    scratch = [vmem(array.shape, array.dtype) for array in given] + [dma((len(given),))]
    scratch += [
        vmem((chunks, 2 * width, cols), F32),
        vmem((chunks, 2 * width, cols), F32),
        vmem((chunks, width, cols), F32),
        vmem((chunks, 5, width, cols), F32),
        vmem((2 * width, cols), F32),
        vmem((2 * width, cols), F32),
        vmem((2, 2 * width, 2 * width), BF16),
        vmem((2, primal, 2 * width), BF16),
        vmem((2, 2 * width, primal), BF16),
        vmem((2, order, 2 * width), BF16),
        vmem((ROUNDS, chunks, 2 * width, cols), F32),
        vmem((ROUNDS, chunks, 2 * width, cols), F32),
        vmem((ROUNDS, chunks, primal, cols), F32),
        vmem((ROUNDS, chunks, others, primal, cols), F32),
        vmem((8, width), F32),
        vmem((8, width), F32),
        vmem((2, 8, loads), F32),
        vmem((2, max(plane - 1, 1), 8, loads), F32),
        vmem((2, max(outer - 1, 1), 8, loads), F32),
        vmem((2, 8, loads), F32),
        dma((chunks,)), dma((chunks,)),
        dma, dma,
        dma((ROUNDS, chunks)), dma((ROUNDS, chunks)),
        dma((ROUNDS, chunks)), dma((ROUNDS, chunks)),
        dma((ROUNDS, chunks, others)), dma((ROUNDS, chunks, others)),
        dma((2, chunks, max(plane - 1, 1))), dma((2, chunks, max(plane - 1, 1))),
        dma((2, max(outer - 1, 1))), dma((2, max(outer - 1, 1))),
    ]
    shape = jax.ShapeDtypeStruct((width, loads), F32)
    mult, resid = pl.pallas_call(
        functools.partial(kernel, subs, grps, inner, chunks),
        out_shape=(shape, shape),
        in_specs=[pl.BlockSpec(memory_space=pl.ANY)] * 9,
        out_specs=(pl.BlockSpec(memory_space=pltpu.VMEM),) * 2,
        scratch_shapes=scratch,
        compiler_params=pltpu.CompilerParams(
            collective_id=0, has_side_effects=True, vmem_limit_bytes=60 * 1024 * 1024
        ),
    )(*given)
    return mult[None, None], resid[None, None]


def solution(mesh):
    sizes = dict(mesh.shape)
    placed = (
        P("sub", "grp", None, None),
        P("sub", "grp", None),
        P("sub", "grp", None),
        P("sub", "grp", None),
        P("sub", "grp", None),
        P("sub", "grp", None, None, None),
        P("sub", "grp", None, None, None),
        P("sub", "grp", None, None, None),
        P("sub", None, None),
    )
    return jax.shard_map(
        functools.partial(local, sizes["sub"], sizes["grp"]),
        mesh=mesh,
        in_specs=placed,
        out_specs=(P("sub", "grp", None, None), P("sub", "grp", None, None)),
        check_vma=False,
    )
```
